32 devices in a mesh: img: 2 (over x), row: 4 (over z), col: 4 (over y, core).
Axes of the slice: x: 2, y: 2, z: 4, core: 2. Of those that a mesh axis runs over, the one named last changes fastest.
Arguments:
- latent: bfloat16 [128, 64, 1280], P(('img', 'row'), 'col'), parts along dimension 0, may hold values from -240 to 240
- norm_gain: float32 [1280], replicated, may hold values from 0.1 to 1.9
- norm_shift: float32 [1280], replicated, may hold values from -3 to 3
- query_weight: bfloat16 [1280, 768], replicated, may hold values from -0.25 to 0.25
- key_weight: bfloat16 [1280, 768], replicated, may hold values from -0.25 to 0.25
- value_weight: bfloat16 [1280, 768], replicated, may hold values from -0.15625 to 0.15625
- output_weight: bfloat16 [768, 1280], replicated, may hold values from -0.875 to 0.875
- output_bias: float32 [1280], replicated, may hold values from -3 to 3
Outputs:
- attended: bfloat16 [128, 64, 1280], P(('img', 'row'), 'col'), parts along dimension 0
The draws below stay inside these ranges and needn't reach their ends.
There are 2 independent parts, one for each index of `img`. The reference program is written for one: setup_inputs(seed, part) draws one part's arguments, and reference() takes and returns one part's arrays. A program takes and returns all parts, laid end to end along the dimension named above; an argument that names none is the same for every part. Nothing has to cross between parts.
All inputs are finite; a program needn't handle non-finite values.
Results may differ from the reference program's by a relative error of at most 0.012.
The reference program's roundings to bfloat16 on the way (of `normed`, `rounded` and `mixed`) count: a program that leaves them out, or rounds other values in their place, can miss the bound.
Values may be sent and summed in bfloat16 or wider, within the bound.
A program may use at most 128 MiB of HBM per device.

```python
import math
import jax
import jax.numpy as jnp
from jax import lax

C = 1280
GROUPS = 32
HD = 64
H = 64
W = 64
CQ = 768


def draw_latent(key, part):
    base = jax.random.fold_in(key, 7)
    key_one, key_two = jax.random.split(base, 2)
    channel_scale = jnp.exp(jax.random.uniform(key_two, (1, 1, C), jnp.float32, 0.0, math.log(10.0)))
    position = jnp.arange(H, dtype=jnp.float32)[:, None, None] / (H - 1)
    group_pick = jax.random.permutation(jax.random.fold_in(base, 23), GROUPS) < GROUPS // 2
    channel_pick = jnp.repeat(group_pick, C // GROUPS)[None, None, :]
    profile = jnp.where(channel_pick, jnp.sqrt(1.0 + 8.0 * position), jnp.sqrt(9.0 - 8.0 * position))
    group_sign = jax.random.rademacher(jax.random.fold_in(base, 31), (GROUPS,), jnp.float32)
    channel_sign = jnp.repeat(group_sign, C // GROUPS)[None, None, :]
    drift = 0.8 * channel_sign * (1.0 + 2.0 * position) * channel_scale
    noise = jax.random.truncated_normal(key_one, -4.0, 4.0, (H, W, C), jnp.float32)
    return jnp.clip(noise * channel_scale * profile + drift, -240.0, 240.0).astype(jnp.bfloat16)


def scatter_about(rng, shape, width, most, kind=jnp.bfloat16):
    entries = width * jax.random.normal(rng, shape, jnp.float32)
    return jnp.clip(entries, min=-most, max=most).astype(kind)


def setup_inputs(seed: int = 0, part: int = 0) -> dict:
    seeds = jax.random.split(jax.random.key(seed), 9)
    part_keys = jax.random.split(jax.random.fold_in(seeds[8], part), 9)
    latent = draw_latent(jax.random.fold_in(jax.random.fold_in(seeds[8], part), 71), part)
    norm_gain = jnp.clip(1.0 + 0.18 * jax.random.normal(seeds[1], (C,), jnp.float32), 0.1, 1.9)
    norm_shift = scatter_about(seeds[2], (C,), 0.5, 3.0, jnp.float32)
    query_weight = scatter_about(seeds[3], (C, CQ), (C // 2) ** -0.5, 0.25)
    key_weight = scatter_about(seeds[4], (C, CQ), (C // 2) ** -0.5, 0.25)
    value_weight = scatter_about(seeds[5], (C, CQ), C ** -0.5, 0.15625)
    output_weight = scatter_about(seeds[6], (CQ, C), (CQ // 16) ** -0.5, 0.875)
    output_bias = scatter_about(seeds[7], (C,), 0.5, 3.0, jnp.float32)
    return dict(latent=latent, norm_gain=norm_gain, norm_shift=norm_shift, query_weight=query_weight, key_weight=key_weight, value_weight=value_weight, output_weight=output_weight, output_bias=output_bias)


def reference(latent, norm_gain, norm_shift, query_weight, key_weight, value_weight, output_weight, output_bias):
    flat = latent.reshape(-1, C).astype(jnp.float32)
    grouped = flat.reshape(flat.shape[0], GROUPS, C // GROUPS)
    mean = lax.optimization_barrier(jnp.mean(grouped, axis=(0, 2)))
    centered = grouped - mean[None, :, None]
    spread = lax.optimization_barrier(jnp.mean(centered * centered, axis=(0, 2)))
    scaled = (centered * lax.rsqrt(spread + 1e-05)[None, :, None]).reshape(-1, C)
    normed = (scaled * norm_gain + norm_shift).astype(jnp.bfloat16)
    queries = jnp.dot(normed, query_weight, preferred_element_type=jnp.float32).astype(jnp.bfloat16)
    keys = jnp.dot(normed, key_weight, preferred_element_type=jnp.float32).astype(jnp.bfloat16)
    values = jnp.dot(normed, value_weight, preferred_element_type=jnp.float32).astype(jnp.bfloat16)
    count = queries.shape[0]
    heads_all = CQ // HD
    scale = 1.0 / math.sqrt(HD)
    block = math.gcd(512, count)
    query_heads = queries.reshape(count, heads_all, HD).transpose(1, 0, 2).astype(jnp.float32)
    key_heads = keys.reshape(count, heads_all, HD).transpose(1, 0, 2).astype(jnp.float32)
    value_heads = values.reshape(count, heads_all, HD).transpose(1, 0, 2).astype(jnp.float32)

    def per_head(items):
        query_one, key_one, value_one = items

        def per_block(query_block):
            scores = jnp.dot(query_block, key_one.T) * scale
            peak = lax.optimization_barrier(jnp.max(scores, axis=1, keepdims=True))
            weights = jnp.exp(scores - peak)
            total = lax.optimization_barrier(jnp.sum(weights, axis=1, keepdims=True))
            rounded = lax.optimization_barrier(weights.astype(jnp.bfloat16)).astype(jnp.float32)
            return jnp.dot(rounded, value_one) / total
        blocks = lax.map(per_block, query_one.reshape(count // block, block, HD))
        return blocks.reshape(count, HD)
    mixed_heads = lax.map(per_head, (query_heads, key_heads, value_heads))
    mixed = mixed_heads.transpose(1, 0, 2).reshape(count, CQ).astype(jnp.bfloat16)
    result = jnp.dot(mixed, output_weight, preferred_element_type=jnp.float32) + output_bias
    return result.astype(jnp.bfloat16).reshape(latent.shape)
```

```python
import functools
import math

import jax
import jax.numpy as jnp
from jax import lax
from jax.experimental import pallas as pl
from jax.experimental.pallas import tpu as pltpu
from jax.sharding import PartitionSpec as P

GROUPS = 32
HD = 64
MESH = pl.DeviceIdType.MESH
F32 = jnp.float32
BF16 = jnp.bfloat16


def xor(a, s):
    out, bit = a, 1
    while bit <= s:
        if s & bit:
            out = out + bit * (1 - 2 * ((a // bit) % 2))
        bit *= 2
    return out


def xor_traced(a, s, n):
    out, bit = 0, 1
    while bit < n:
        out = out + bit * (((a // bit) + (s // bit)) % 2)
        bit *= 2
    return out


def kernel(
    ax_a, ax_b, na, nb, tok, width, wide_heads, per,
    x_hbm, gain_ref, shift_ref, wq_hbm, wk_hbm, wv_hbm, wo_hbm, bias_ref,
    out_ref,
    x_v, wq, wk, wv, wo, stat_own, stat_in, q_own, q_in, kv_own, kv, qh, m_s, acc, mix_out, mix_in,
    load_sem, own_sem, st_send, st_recv, q_send, q_recv, z_send, z_recv, f_send, f_recv, o_send, o_recv,
):
    me_a = lax.axis_index(ax_a)
    me_b = lax.axis_index(ax_b)
    gw = per * HD
    padw = kv.shape[-1]
    everyone = [(s, t) for s in range(na) for t in range(nb) if s or t]

    def dev(s, t):
        return {ax_a: xor(me_a, s), ax_b: xor(me_b, t)}

    def remote(src, dst, ssem, rsem, where):
        return pltpu.make_async_remote_copy(
            src_ref=src, dst_ref=dst, send_sem=ssem, recv_sem=rsem, device_id=where, device_id_type=MESH
        )

    loads = [
        pltpu.make_async_copy(a, b, load_sem.at[i])
        for i, (a, b) in enumerate(((x_hbm, x_v), (wq_hbm, wq), (wk_hbm, wk), (wv_hbm, wv), (wo_hbm, wo)))
    ]
    for copy in loads:
        copy.start()
    barrier = pltpu.get_barrier_semaphore()
    for s, t in everyone:
        pl.semaphore_signal(barrier, inc=1, device_id=dev(s, t), device_id_type=MESH)

    size = width // GROUPS
    chan = lax.broadcasted_iota(jnp.int32, (width, 128), 0)
    lane = lax.broadcasted_iota(jnp.int32, (width, 128), 1)
    gather = jnp.where((chan >= lane * size) & (chan < lane * size + size), 1.0, 0.0).astype(F32)
    chan_t = lax.broadcasted_iota(jnp.int32, (128, width), 1)
    lane_t = lax.broadcasted_iota(jnp.int32, (128, width), 0)
    spread = jnp.where((chan_t >= lane_t * size) & (chan_t < lane_t * size + size), 1.0, 0.0).astype(F32)

    def to_groups(row):
        return jnp.dot(
            jnp.broadcast_to(row, (8, width)), gather, preferred_element_type=F32, precision=lax.Precision.HIGHEST
        )[:1]

    def to_channels(row):
        return jnp.dot(
            jnp.broadcast_to(row, (8, 128)), spread, preferred_element_type=F32, precision=lax.Precision.HIGHEST
        )[:1]

    loads[0].wait()
    x = x_v[...].astype(F32)
    here = float(tok * size)
    mean_here = to_groups(jnp.sum(x, axis=0, keepdims=True)) / here
    off = x - to_channels(mean_here)
    dev_here = to_groups(jnp.sum(off * off, axis=0, keepdims=True))
    stat_own[...] = jnp.concatenate([mean_here, dev_here, jnp.zeros((6, 128), F32)], axis=0)
    pl.semaphore_wait(barrier, len(everyone))
    stats = []
    for s, t in everyone:
        i = s * nb + t
        copy = remote(stat_own, stat_in.at[i], st_send.at[i], st_recv.at[i], dev(s, t))
        copy.start()
        stats.append(copy)
    for copy in stats:
        copy.wait()
    means = [stat_own[0:1, :]] + [stat_in[s * nb + t, 0:1, :] for s, t in everyone]
    devs = [stat_own[1:2, :]] + [stat_in[s * nb + t, 1:2, :] for s, t in everyone]
    mean = sum(means) / float(na * nb)
    total_dev = sum(devs) + here * sum((m - mean) * (m - mean) for m in means)
    rstd = lax.rsqrt(total_dev / (here * na * nb) + 1e-05)
    mean_c = to_channels(mean)
    rstd_c = to_channels(rstd)
    normed = ((x_v[...].astype(F32) - mean_c) * rstd_c * gain_ref[...] + shift_ref[...]).astype(BF16)

    loads[1].wait()
    q = jnp.dot(normed, wq[...], preferred_element_type=F32) * (math.log2(math.e) / math.sqrt(HD))
    q = q.astype(BF16).astype(F32).T.astype(BF16)
    for g in range(na):
        q_own[g] = q[g * gw : (g + 1) * gw]
    q_copies = [
        remote(q_own.at[xor(me_a, s)], q_in.at[s - 1], q_send.at[s - 1], q_recv.at[s - 1], dev(s, 0))
        for s in range(1, na)
    ]
    for copy in q_copies:
        copy.start()
    loads[2].wait()
    k = jnp.dot(normed, wk[...], preferred_element_type=F32)
    k = k.astype(BF16).astype(F32).T.astype(BF16)
    for g in range(na):
        kv_own[g, 0:gw, :] = k[g * gw : (g + 1) * gw]
    loads[3].wait()
    v = jnp.dot(normed, wv[...], preferred_element_type=F32)
    for g in range(na):
        part = jnp.concatenate([v[:, g * gw : (g + 1) * gw], jnp.ones((tok, padw - gw), F32)], axis=1)
        kv_own[g, gw : gw + tok, :] = part.astype(BF16)
    z_copies = [
        remote(kv_own.at[xor(me_a, s)], kv.at[s, 0], z_send.at[s - 1], z_recv.at[s - 1], dev(s, 0))
        for s in range(1, na)
    ]
    for copy in z_copies:
        copy.start()
    own = pltpu.make_async_copy(kv_own.at[me_a], kv.at[0, 0], own_sem)
    own.start()

    def forward(s, t):
        src = kv.at[s, t - 1] if t % 2 and t > 1 else kv.at[s, 0]
        hop = 1 if t % 2 else t
        return remote(src, kv.at[s, t], f_send.at[s, t], f_recv.at[s, t], dev(0, hop))

    direct = [t for t in range(1, nb) if t == 1 or t % 2 == 0]
    relayed = [t for t in range(3, nb, 2)]

    def first(s):
        if s == 0:
            own.wait()
        else:
            z_copies[s - 1].wait()
        for t in reversed(direct):
            forward(s, t).start()

    def second(s):
        for t in relayed:
            forward(s, t - 1).wait_recv()
            forward(s, t).start()

    def third(s):
        for t in range(1, nb):
            if t + 1 not in relayed:
                forward(s, t).wait_recv()

    def unpack(i, block):
        for h in range(per):
            qh[h, i] = block[h * HD : (h + 1) * HD].astype(F32).T.astype(BF16)

    def compute(s, i, h):
        rows = pl.ds(pl.multiple_of(h * HD, HD), HD)
        query = qh[h, i]
        scores = [
            jnp.dot(query, kv[s, t, rows, :], preferred_element_type=F32) for t in range(nb)
        ]
        peak = functools.reduce(jnp.maximum, scores)
        peak = jnp.max(peak, axis=1, keepdims=True)
        if s:
            old = m_s[h, i][:, :1]
            peak = jnp.maximum(peak, old)
        mixed = None
        for t in range(nb):
            rounded = jnp.exp2(scores[t] - peak).astype(BF16)
            piece = jnp.dot(rounded, kv[s, t, gw : gw + tok, :], preferred_element_type=F32)
            mixed = piece if mixed is None else mixed + piece
        if s:
            mixed = acc[h, i] * jnp.exp2(old - peak) + mixed
        acc[h, i] = mixed
        if s < na - 1:
            m_s[h, i] = jnp.broadcast_to(peak, (tok, 128))

    def run(s, low, high):
        def step(j, c):
            compute(s, j // per, j % per)
            return c

        lax.fori_loop(low * per, high * per, step, 0)

    def finish(i):
        parts = []
        for h in range(per):
            a = acc[h, i]
            parts.append(a[:, h * HD : (h + 1) * HD] / a[:, gw : gw + 1])
        return jnp.concatenate(parts, axis=1).astype(BF16).astype(F32).T.astype(BF16)

    first(0)
    unpack(0, q_own[me_a])
    second(0)
    third(0)
    half = na // 2
    for s in range(na):
        if s == 0:
            run(0, 0, 1)
            for i in range(1, na):
                q_copies[i - 1].wait()
                unpack(i, q_in[i - 1])
            first(1)
            run(0, 1, half + 1)
            second(1)
            run(0, half + 1, na)
            third(1)
        elif s < na - 1:
            run(s, 0, half)
            first(s + 1)
            second(s + 1)
            run(s, half, na)
            third(s + 1)

    last = na - 1

    def back(j, c):
        i = last - j
        lax.fori_loop(0, per, lambda h, d: (compute(last, i, h), d)[1], 0)
        mix_out[i] = finish(i)
        remote(
            mix_out.at[i],
            mix_in.at[pl.ds(pl.multiple_of(me_a * gw, gw), gw)],
            o_send.at[i],
            o_recv.at[i],
            {ax_a: xor_traced(me_a, i, na), ax_b: me_b},
        ).start()
        return c

    lax.fori_loop(0, last, back, 0)
    lax.fori_loop(0, per, lambda h, d: (compute(last, 0, h), d)[1], 0)
    mix_in[pl.ds(pl.multiple_of(me_a * gw, gw), gw), :] = finish(0)
    loads[4].wait()
    for s in range(na):
        for t in range(1, nb):
            forward(s, t).wait_send()
    for i in range(1, na):
        copy = remote(
            mix_out.at[i],
            mix_in.at[pl.ds(pl.multiple_of(xor(me_a, i) * gw, gw), gw)],
            o_send.at[i],
            o_recv.at[i],
            dev(i, 0),
        )
        copy.wait()
    mixed = mix_in[...].astype(F32).T.astype(BF16)
    result = jnp.dot(mixed, wo[...], preferred_element_type=F32) + bias_ref[...]
    out_ref[...] = result.astype(BF16)


def local(sizes, latent, gain, shift, wq, wk, wv, wo, bias):
    rows, cols, width = latent.shape
    tok = rows * cols
    wide = wq.shape[1]
    heads = wide // HD
    ax_a, ax_b = ("row", "col") if heads % sizes["row"] == 0 else ("col", "row")
    na, nb = sizes[ax_a], sizes[ax_b]
    per = heads // na
    gw = per * HD
    padw = (gw // 128 + 1) * 128
    assert padw == tok
    vm = pltpu.VMEM
    dma = pltpu.SemaphoreType.DMA
    anyspec = pl.BlockSpec(memory_space=pl.ANY)
    vspec = pl.BlockSpec(memory_space=pltpu.VMEM)
    out = pl.pallas_call(
        functools.partial(kernel, ax_a, ax_b, na, nb, tok, width, heads, per),
        out_shape=jax.ShapeDtypeStruct((tok, width), BF16),
        in_specs=[anyspec, vspec, vspec, anyspec, anyspec, anyspec, anyspec, vspec],
        out_specs=vspec,
        scratch_shapes=[
            vm((tok, width), BF16),
            vm((width, wide), BF16),
            vm((width, wide), BF16),
            vm((width, wide), BF16),
            vm((wide, width), BF16),
            vm((8, 128), F32),
            vm((na * nb, 8, 128), F32),
            vm((na, gw, tok), BF16),
            vm((na - 1, gw, tok), BF16),
            vm((na, gw + tok, padw), BF16),
            vm((na, nb, gw + tok, padw), BF16),
            vm((per, na, tok, HD), BF16),
            vm((per, na, tok, 128), F32),
            vm((per, na, tok, padw), F32),
            vm((na, gw, tok), BF16),
            vm((wide, tok), BF16),
            dma((5,)),
            dma,
            dma((na * nb,)),
            dma((na * nb,)),
            dma((na - 1,)),
            dma((na - 1,)),
            dma((na - 1,)),
            dma((na - 1,)),
            dma((na, nb)),
            dma((na, nb)),
            dma((na,)),
            dma((na,)),
        ],
        compiler_params=pltpu.CompilerParams(
            collective_id=0, has_side_effects=True, vmem_limit_bytes=56 * 1024 * 1024
        ),
    )(
        latent.reshape(tok, width), gain.reshape(1, width), shift.reshape(1, width),
        wq, wk, wv, wo, bias.reshape(1, width),
    )
    return out.reshape(rows, cols, width)


def solution(mesh):
    placed = (P(("img", "row"), "col", None), P(), P(), P(), P(), P(), P(), P())
    return jax.shard_map(
        functools.partial(local, dict(mesh.shape)),
        mesh=mesh, in_specs=placed, out_specs=P(("img", "row"), "col", None), check_vma=False,
    )
```

```python
import functools
import math

import jax
import jax.numpy as jnp
from jax import lax
from jax.experimental import pallas as pl
from jax.experimental.pallas import tpu as pltpu
from jax.sharding import PartitionSpec as P

GROUPS = 32
HD = 64
MESH = pl.DeviceIdType.MESH
F32 = jnp.float32
BF16 = jnp.bfloat16


def xor(a, s):
    out, bit = a, 1
    while bit <= s:
        if s & bit:
            out = out + bit * (1 - 2 * ((a // bit) % 2))
        bit *= 2
    return out


def xor_traced(a, s, n):
    out, bit = 0, 1
    while bit < n:
        out = out + bit * (((a // bit) + (s // bit)) % 2)
        bit *= 2
    return out


def kernel(
    ax_a, ax_b, na, nb, tok, width, wide_heads, per,
    x_hbm, gain_ref, shift_ref, wq_hbm, wk_hbm, wv_hbm, wo_hbm, bias_ref,
    out_ref,
    x_v, wq, wk, wv, wo, stat_own, stat_in, q_own, q_in, kv_own, kv, qh, m_s, acc, mix_out, mix_in,
    load_sem, own_sem, st_send, st_recv, q_send, q_recv, z_send, z_recv, f_send, f_recv, o_send, o_recv,
):
    me_a = lax.axis_index(ax_a)
    me_b = lax.axis_index(ax_b)
    gw = per * HD
    padw = kv.shape[-1]
    everyone = [(s, t) for s in range(na) for t in range(nb) if s or t]

    def dev(s, t):
        return {ax_a: xor(me_a, s), ax_b: xor(me_b, t)}

    def remote(src, dst, ssem, rsem, where):
        return pltpu.make_async_remote_copy(
            src_ref=src, dst_ref=dst, send_sem=ssem, recv_sem=rsem, device_id=where, device_id_type=MESH
        )

    loads = [
        pltpu.make_async_copy(a, b, load_sem.at[i])
        for i, (a, b) in enumerate(((x_hbm, x_v), (wq_hbm, wq), (wk_hbm, wk), (wv_hbm, wv), (wo_hbm, wo)))
    ]
    for copy in loads:
        copy.start()
    barrier = pltpu.get_barrier_semaphore()
    for s, t in everyone:
        pl.semaphore_signal(barrier, inc=1, device_id=dev(s, t), device_id_type=MESH)

    size = width // GROUPS
    chan = lax.broadcasted_iota(jnp.int32, (width, 128), 0)
    lane = lax.broadcasted_iota(jnp.int32, (width, 128), 1)
    gather = jnp.where((chan >= lane * size) & (chan < lane * size + size), 1.0, 0.0).astype(F32)
    chan_t = lax.broadcasted_iota(jnp.int32, (128, width), 1)
    lane_t = lax.broadcasted_iota(jnp.int32, (128, width), 0)
    spread = jnp.where((chan_t >= lane_t * size) & (chan_t < lane_t * size + size), 1.0, 0.0).astype(F32)

    def to_groups(row):
        return jnp.dot(
            jnp.broadcast_to(row, (8, width)), gather, preferred_element_type=F32, precision=lax.Precision.HIGHEST
        )[:1]

    def to_channels(row):
        return jnp.dot(
            jnp.broadcast_to(row, (8, 128)), spread, preferred_element_type=F32, precision=lax.Precision.HIGHEST
        )[:1]

    loads[0].wait()
    x = x_v[...].astype(F32)
    here = float(tok * size)
    mean_here = to_groups(jnp.sum(x, axis=0, keepdims=True)) / here
    off = x - to_channels(mean_here)
    dev_here = to_groups(jnp.sum(off * off, axis=0, keepdims=True))
    stat_own[...] = jnp.concatenate([mean_here, dev_here, jnp.zeros((6, 128), F32)], axis=0)
    pl.semaphore_wait(barrier, len(everyone))
    stats = []
    for s, t in everyone:
        i = s * nb + t
        copy = remote(stat_own, stat_in.at[i], st_send.at[i], st_recv.at[i], dev(s, t))
        copy.start()
        stats.append(copy)
    for copy in stats:
        copy.wait()
    means = [stat_own[0:1, :]] + [stat_in[s * nb + t, 0:1, :] for s, t in everyone]
    devs = [stat_own[1:2, :]] + [stat_in[s * nb + t, 1:2, :] for s, t in everyone]
    mean = sum(means) / float(na * nb)
    total_dev = sum(devs) + here * sum((m - mean) * (m - mean) for m in means)
    rstd = lax.rsqrt(total_dev / (here * na * nb) + 1e-05)
    mean_c = to_channels(mean)
    rstd_c = to_channels(rstd)
    normed = ((x_v[...].astype(F32) - mean_c) * rstd_c * gain_ref[...][None, :] + shift_ref[...][None, :]).astype(BF16)

    loads[1].wait()
    q = jnp.dot(normed, wq[...], preferred_element_type=F32) * (math.log2(math.e) / math.sqrt(HD))
    q = q.astype(BF16).astype(F32).T.astype(BF16)
    for g in range(na):
        q_own[g] = q[g * gw : (g + 1) * gw]
    q_copies = [
        remote(q_own.at[xor(me_a, s)], q_in.at[s - 1], q_send.at[s - 1], q_recv.at[s - 1], dev(s, 0))
        for s in range(1, na)
    ]
    for copy in q_copies:
        copy.start()
    loads[2].wait()
    k = jnp.dot(normed, wk[...], preferred_element_type=F32)
    k = k.astype(BF16).astype(F32).T.astype(BF16)
    for g in range(na):
        kv_own[g, 0:gw, :] = k[g * gw : (g + 1) * gw]
    loads[3].wait()
    v = jnp.dot(normed, wv[...], preferred_element_type=F32)
    for g in range(na):
        part = jnp.concatenate([v[:, g * gw : (g + 1) * gw], jnp.ones((tok, padw - gw), F32)], axis=1)
        kv_own[g, gw : gw + tok, :] = part.astype(BF16)
    z_copies = [
        remote(kv_own.at[xor(me_a, s)], kv.at[s, 0], z_send.at[s - 1], z_recv.at[s - 1], dev(s, 0))
        for s in range(1, na)
    ]
    for copy in z_copies:
        copy.start()
    own = pltpu.make_async_copy(kv_own.at[me_a], kv.at[0, 0], own_sem)
    own.start()

    def forward(s, t):
        src = kv.at[s, t - 1] if t % 2 and t > 1 else kv.at[s, 0]
        hop = 1 if t % 2 else t
        return remote(src, kv.at[s, t], f_send.at[s, t], f_recv.at[s, t], dev(0, hop))

    direct = [t for t in range(1, nb) if t == 1 or t % 2 == 0]
    relayed = [t for t in range(3, nb, 2)]

    def first(s):
        if s == 0:
            own.wait()
        else:
            z_copies[s - 1].wait()
        for t in reversed(direct):
            forward(s, t).start()

    def second(s):
        for t in relayed:
            forward(s, t - 1).wait_recv()
            forward(s, t).start()

    def third(s):
        for t in range(1, nb):
            if t + 1 not in relayed:
                forward(s, t).wait_recv()

    def unpack(i, block):
        for h in range(per):
            qh[h, i] = block[h * HD : (h + 1) * HD].astype(F32).T.astype(BF16)

    def score(s, i, h):
        query = qh[h, i]
        return [
            jnp.dot(query, kv[s, t, h * HD : (h + 1) * HD, :], preferred_element_type=F32) for t in range(nb)
        ]

    def absorb(s, i, h, scores):
        peak = functools.reduce(jnp.maximum, scores)
        peak = jnp.max(peak, axis=1, keepdims=True)
        if s:
            old = m_s[h, i][:, :1]
            peak = jnp.maximum(peak, old)
        mixed = None
        for t in range(nb):
            rounded = jnp.exp2(scores[t] - peak).astype(BF16)
            piece = jnp.dot(rounded, kv[s, t, gw : gw + tok, :], preferred_element_type=F32)
            mixed = piece if mixed is None else mixed + piece
        if s:
            mixed = acc[h, i] * jnp.exp2(old - peak) + mixed
        acc[h, i] = mixed
        if s < na - 1:
            m_s[h, i] = jnp.broadcast_to(peak, (tok, 128))

    def compute(s, i):
        scores = score(s, i, 0)
        for h in range(per):
            later = score(s, i, h + 1) if h + 1 < per else None
            absorb(s, i, h, scores)
            scores = later

    def run(s, low, high):
        lax.fori_loop(low, high, lambda i, c: (compute(s, i), c)[1], 0)

    def finish(i):
        parts = []
        for h in range(per):
            a = acc[h, i]
            parts.append(a[:, h * HD : (h + 1) * HD] / a[:, gw : gw + 1])
        return jnp.concatenate(parts, axis=1).astype(BF16).astype(F32).T.astype(BF16)

    first(0)
    unpack(0, q_own[me_a])
    second(0)
    third(0)
    half = na // 2
    for s in range(na):
        if s == 0:
            run(0, 0, 1)
            for i in range(1, na):
                q_copies[i - 1].wait()
                unpack(i, q_in[i - 1])
            first(1)
            run(0, 1, half + 1)
            second(1)
            run(0, half + 1, na)
            third(1)
        elif s < na - 1:
            run(s, 0, half)
            first(s + 1)
            second(s + 1)
            run(s, half, na)
            third(s + 1)

    last = na - 1

    def back(j, c):
        i = last - j
        compute(last, i)
        mix_out[i] = finish(i)
        remote(
            mix_out.at[i],
            mix_in.at[pl.ds(pl.multiple_of(me_a * gw, gw), gw)],
            o_send.at[i],
            o_recv.at[i],
            {ax_a: xor_traced(me_a, i, na), ax_b: me_b},
        ).start()
        return c

    lax.fori_loop(0, last, back, 0)
    compute(last, 0)
    mix_in[pl.ds(pl.multiple_of(me_a * gw, gw), gw), :] = finish(0)
    loads[4].wait()
    for s in range(na):
        for t in range(1, nb):
            forward(s, t).wait_send()
    for i in range(1, na):
        copy = remote(
            mix_out.at[i],
            mix_in.at[pl.ds(pl.multiple_of(xor(me_a, i) * gw, gw), gw)],
            o_send.at[i],
            o_recv.at[i],
            dev(i, 0),
        )
        copy.wait()
    mixed = mix_in[...].astype(F32).T.astype(BF16)
    result = jnp.dot(mixed, wo[...], preferred_element_type=F32) + bias_ref[...][None, :]
    out_ref[...] = result.astype(BF16)


def local(sizes, latent, gain, shift, wq, wk, wv, wo, bias):
    rows, cols, width = latent.shape
    tok = rows * cols
    wide = wq.shape[1]
    heads = wide // HD
    ax_a, ax_b = ("row", "col") if heads % sizes["row"] == 0 else ("col", "row")
    na, nb = sizes[ax_a], sizes[ax_b]
    per = heads // na
    gw = per * HD
    padw = (gw // 128 + 1) * 128
    assert padw == tok
    vm = pltpu.VMEM
    dma = pltpu.SemaphoreType.DMA
    anyspec = pl.BlockSpec(memory_space=pl.ANY)
    vspec = pl.BlockSpec(memory_space=pltpu.VMEM)
    out = pl.pallas_call(
        functools.partial(kernel, ax_a, ax_b, na, nb, tok, width, heads, per),
        out_shape=jax.ShapeDtypeStruct((tok, width), BF16),
        in_specs=[anyspec, vspec, vspec, anyspec, anyspec, anyspec, anyspec, vspec],
        out_specs=vspec,
        scratch_shapes=[
            vm((tok, width), BF16),
            vm((width, wide), BF16),
            vm((width, wide), BF16),
            vm((width, wide), BF16),
            vm((wide, width), BF16),
            vm((8, 128), F32),
            vm((na * nb, 8, 128), F32),
            vm((na, gw, tok), BF16),
            vm((na - 1, gw, tok), BF16),
            vm((na, gw + tok, padw), BF16),
            vm((na, nb, gw + tok, padw), BF16),
            vm((per, na, tok, HD), BF16),
            vm((per, na, tok, 128), F32),
            vm((per, na, tok, padw), F32),
            vm((na, gw, tok), BF16),
            vm((wide, tok), BF16),
            dma((5,)),
            dma,
            dma((na * nb,)),
            dma((na * nb,)),
            dma((na - 1,)),
            dma((na - 1,)),
            dma((na - 1,)),
            dma((na - 1,)),
            dma((na, nb)),
            dma((na, nb)),
            dma((na,)),
            dma((na,)),
        ],
        compiler_params=pltpu.CompilerParams(
            collective_id=0, has_side_effects=True, vmem_limit_bytes=56 * 1024 * 1024
        ),
    )(
        latent.reshape(tok, width), gain, shift, wq, wk, wv, wo, bias,
    )
    return out.reshape(rows, cols, width)


def solution(mesh):
    placed = (P(("img", "row"), "col", None), P(), P(), P(), P(), P(), P(), P())
    return jax.shard_map(
        functools.partial(local, dict(mesh.shape)),
        mesh=mesh, in_specs=placed, out_specs=P(("img", "row"), "col", None), check_vma=False,
    )
```

```python
import functools
import math

import jax
import jax.numpy as jnp
from jax import lax
from jax.experimental import pallas as pl
from jax.experimental.pallas import tpu as pltpu
from jax.sharding import PartitionSpec as P

GROUPS = 32
HD = 64
MESH = pl.DeviceIdType.MESH
F32 = jnp.float32
BF16 = jnp.bfloat16


def xor(a, s):
    out, bit = a, 1
    while bit <= s:
        if s & bit:
            out = out + bit * (1 - 2 * ((a // bit) % 2))
        bit *= 2
    return out


def xor_traced(a, s, n):
    out, bit = 0, 1
    while bit < n:
        out = out + bit * (((a // bit) + (s // bit)) % 2)
        bit *= 2
    return out


def kernel(
    ax_a, ax_b, na, nb, tok, width, wide_heads, per,
    x_hbm, gain_ref, shift_ref, wq_hbm, wk_hbm, wv_hbm, wo_hbm, bias_ref,
    out_ref,
    x_v, wq, wk, wv, wo, stat_own, stat_in, q_own, q_in, k_own, v_own, kbuf, vbuf, v_full, qh, m_s, acc, mix_out, mix_in,
    load_sem, own_sem, st_send, st_recv, q_send, q_recv, z_send, z_recv, f_send, f_recv, o_send, o_recv,
):
    me_a = lax.axis_index(ax_a)
    me_b = lax.axis_index(ax_b)
    gw = per * HD
    padw = v_full.shape[-1]
    whole, half_tok = gw // 128, tok // 2
    everyone = [(s, t) for s in range(na) for t in range(nb) if s or t]

    def dev(s, t):
        return {ax_a: xor(me_a, s), ax_b: xor(me_b, t)}

    def remote(src, dst, ssem, rsem, where):
        return pltpu.make_async_remote_copy(
            src_ref=src, dst_ref=dst, send_sem=ssem, recv_sem=rsem, device_id=where, device_id_type=MESH
        )

    loads = [
        pltpu.make_async_copy(a, b, load_sem.at[i])
        for i, (a, b) in enumerate(((x_hbm, x_v), (wq_hbm, wq), (wk_hbm, wk), (wv_hbm, wv), (wo_hbm, wo)))
    ]
    for copy in loads:
        copy.start()
    barrier = pltpu.get_barrier_semaphore()
    for s, t in everyone:
        pl.semaphore_signal(barrier, inc=1, device_id=dev(s, t), device_id_type=MESH)

    size = width // GROUPS
    chan = lax.broadcasted_iota(jnp.int32, (width, 128), 0)
    lane = lax.broadcasted_iota(jnp.int32, (width, 128), 1)
    gather = jnp.where((chan >= lane * size) & (chan < lane * size + size), 1.0, 0.0).astype(F32)
    chan_t = lax.broadcasted_iota(jnp.int32, (128, width), 1)
    lane_t = lax.broadcasted_iota(jnp.int32, (128, width), 0)
    spread = jnp.where((chan_t >= lane_t * size) & (chan_t < lane_t * size + size), 1.0, 0.0).astype(F32)

    def to_groups(row):
        return jnp.dot(
            jnp.broadcast_to(row, (8, width)), gather, preferred_element_type=F32, precision=lax.Precision.HIGHEST
        )[:1]

    def to_channels(row):
        return jnp.dot(
            jnp.broadcast_to(row, (8, 128)), spread, preferred_element_type=F32, precision=lax.Precision.HIGHEST
        )[:1]

    loads[0].wait()
    x = x_v[...].astype(F32)
    here = float(tok * size)
    mean_here = to_groups(jnp.sum(x, axis=0, keepdims=True)) / here
    off = x - to_channels(mean_here)
    dev_here = to_groups(jnp.sum(off * off, axis=0, keepdims=True))
    stat_own[...] = jnp.concatenate([mean_here, dev_here, jnp.zeros((6, 128), F32)], axis=0)
    pl.semaphore_wait(barrier, len(everyone))
    stats = []
    for s, t in everyone:
        i = s * nb + t
        copy = remote(stat_own, stat_in.at[i], st_send.at[i], st_recv.at[i], dev(s, t))
        copy.start()
        stats.append(copy)
    for copy in stats:
        copy.wait()
    means = [stat_own[0:1, :]] + [stat_in[s * nb + t, 0:1, :] for s, t in everyone]
    devs = [stat_own[1:2, :]] + [stat_in[s * nb + t, 1:2, :] for s, t in everyone]
    mean = sum(means) / float(na * nb)
    total_dev = sum(devs) + here * sum((m - mean) * (m - mean) for m in means)
    rstd = lax.rsqrt(total_dev / (here * na * nb) + 1e-05)
    mean_c = to_channels(mean)
    rstd_c = to_channels(rstd)
    normed = ((x_v[...].astype(F32) - mean_c) * rstd_c * gain_ref[...][None, :] + shift_ref[...][None, :]).astype(BF16)

    loads[1].wait()
    q = jnp.dot(normed, wq[...], preferred_element_type=F32) * (math.log2(math.e) / math.sqrt(HD))
    q = q.astype(BF16).astype(F32).T.astype(BF16)
    for g in range(na):
        q_own[g] = q[g * gw : (g + 1) * gw]
    q_copies = [
        remote(q_own.at[xor(me_a, s)], q_in.at[s - 1], q_send.at[s - 1], q_recv.at[s - 1], dev(s, 0))
        for s in range(1, na)
    ]
    for copy in q_copies:
        copy.start()
    loads[2].wait()
    k = jnp.dot(normed, wk[...], preferred_element_type=F32)
    k = k.astype(BF16).astype(F32).T.astype(BF16)
    for g in range(na):
        k_own[g] = k[g * gw : (g + 1) * gw]
    loads[3].wait()
    v = jnp.dot(normed, wv[...], preferred_element_type=F32)
    for g in range(na):
        part = v[:, g * gw : (g + 1) * gw].astype(BF16).astype(F32)
        for n in range(whole):
            v_own[g, n * tok : (n + 1) * tok, :] = part[:, n * 128 : (n + 1) * 128].astype(BF16)
        rest = part[:, whole * 128 :]
        folded = jnp.concatenate([rest[:half_tok], rest[half_tok:]], axis=1)
        v_own[g, whole * tok :, :] = folded.astype(BF16)
    owned, landed = (k_own, v_own), (kbuf, vbuf)

    def exchange(s, p):
        return remote(
            owned[p].at[xor(me_a, s)], landed[p].at[s, 0], z_send.at[s - 1, p], z_recv.at[s - 1, p], dev(s, 0)
        )

    for p in range(2):
        for s in (3, 1):
            exchange(s, p).start()
    own = [pltpu.make_async_copy(owned[p].at[me_a], landed[p].at[0, 0], own_sem.at[p]) for p in range(2)]
    for copy in own:
        copy.start()

    def forward(s, t, p):
        buf = landed[p]
        src = buf.at[s, t - 1] if t % 2 and t > 1 else buf.at[s, 0]
        hop = 1 if t % 2 else t
        return remote(src, buf.at[s, t], f_send.at[s, t, p], f_recv.at[s, t, p], dev(0, hop))

    direct = [t for t in range(1, nb) if t == 1 or t % 2 == 0]
    relayed = [t for t in range(3, nb, 2)]

    def first(s):
        for p in range(2):
            if s == 0:
                own[p].wait()
            else:
                exchange(s, p).wait_recv()
            for t in reversed(direct):
                forward(s, t, p).start()

    def second(s):
        for p in range(2):
            for t in relayed:
                forward(s, t - 1, p).wait_recv()
                forward(s, t, p).start()

    def third(s):
        for t in range(nb):
            for p in range(2):
                if t and t + 1 not in relayed:
                    forward(s, t, p).wait_recv()
            for n in range(whole):
                v_full[t, :, n * 128 : (n + 1) * 128] = vbuf[s, t, n * tok : (n + 1) * tok, :]
            folded = vbuf[s, t, whole * tok :, :].astype(F32)
            lower = jnp.concatenate([folded[:, :HD], jnp.ones((half_tok, 128 - HD), F32)], axis=1)
            upper = jnp.concatenate([folded[:, HD:], jnp.ones((half_tok, 128 - HD), F32)], axis=1)
            v_full[t, :half_tok, whole * 128 :] = lower.astype(BF16)
            v_full[t, half_tok:, whole * 128 :] = upper.astype(BF16)

    def unpack(i, block):
        for h in range(per):
            qh[h, i] = block[h * HD : (h + 1) * HD].astype(F32).T.astype(BF16)

    def score(s, i, h):
        query = qh[h, i]
        return [
            jnp.dot(query, kbuf[s, t, h * HD : (h + 1) * HD, :], preferred_element_type=F32) for t in range(nb)
        ]

    def absorb(s, i, h, scores):
        peak = functools.reduce(jnp.maximum, scores)
        peak = jnp.max(peak, axis=1, keepdims=True)
        if s:
            old = m_s[h, i][:, :1]
            peak = jnp.maximum(peak, old)
        mixed = None
        for t in range(nb):
            rounded = jnp.exp2(scores[t] - peak).astype(BF16)
            piece = jnp.dot(rounded, v_full[t], preferred_element_type=F32)
            mixed = piece if mixed is None else mixed + piece
        if s:
            mixed = acc[h, i] * jnp.exp2(old - peak) + mixed
        acc[h, i] = mixed
        if s != last:
            m_s[h, i] = jnp.broadcast_to(peak, (tok, 128))

    def compute(s, i):
        scores = score(s, i, 0)
        for h in range(per):
            later = score(s, i, h + 1) if h + 1 < per else None
            absorb(s, i, h, scores)
            scores = later

    def run(s, low, high):
        lax.fori_loop(low, high, lambda i, c: (compute(s, i), c)[1], 0)

    def finish(i):
        parts = []
        for h in range(per):
            a = acc[h, i]
            parts.append(a[:, h * HD : (h + 1) * HD] / a[:, gw : gw + 1])
        return jnp.concatenate(parts, axis=1).astype(BF16).astype(F32).T.astype(BF16)

    last = 2
    first(0)
    unpack(0, q_own[me_a])
    second(0)
    third(0)
    run(0, 0, 1)
    for i in range(1, na):
        q_copies[i - 1].wait()
        unpack(i, q_in[i - 1])
    run(0, 1, 2)
    first(1)
    run(0, 2, 3)
    first(3)
    for p in range(2):
        exchange(2, p).start()
    second(1)
    run(0, 3, 4)
    second(3)
    third(1)
    run(1, 0, 4)
    first(2)
    third(3)
    run(3, 0, 2)
    second(2)
    run(3, 2, 4)
    third(2)

    def back(j, c):
        i = na - 1 - j
        compute(last, i)
        mix_out[i] = finish(i)
        remote(
            mix_out.at[i],
            mix_in.at[pl.ds(pl.multiple_of(me_a * gw, gw), gw)],
            o_send.at[i],
            o_recv.at[i],
            {ax_a: xor_traced(me_a, i, na), ax_b: me_b},
        ).start()
        return c

    lax.fori_loop(0, na - 1, back, 0)
    compute(last, 0)
    mix_in[pl.ds(pl.multiple_of(me_a * gw, gw), gw), :] = finish(0)
    loads[4].wait()
    for p in range(2):
        for s in range(na):
            if s:
                exchange(s, p).wait_send()
            for t in range(1, nb):
                forward(s, t, p).wait_send()
    for i in range(1, na):
        copy = remote(
            mix_out.at[i],
            mix_in.at[pl.ds(pl.multiple_of(xor(me_a, i) * gw, gw), gw)],
            o_send.at[i],
            o_recv.at[i],
            dev(i, 0),
        )
        copy.wait()
    mixed = mix_in[...].astype(F32).T.astype(BF16)
    result = jnp.dot(mixed, wo[...], preferred_element_type=F32) + bias_ref[...][None, :]
    out_ref[...] = result.astype(BF16)


def local(sizes, latent, gain, shift, wq, wk, wv, wo, bias):
    rows, cols, width = latent.shape
    tok = rows * cols
    wide = wq.shape[1]
    heads = wide // HD
    ax_a, ax_b = ("row", "col") if heads % sizes["row"] == 0 else ("col", "row")
    na, nb = sizes[ax_a], sizes[ax_b]
    per = heads // na
    gw = per * HD
    padw = (gw // 128 + 1) * 128
    assert na == 4 and gw % 128 == HD
    vrows = tok * (gw // 128) + tok // 2
    vm = pltpu.VMEM
    dma = pltpu.SemaphoreType.DMA
    anyspec = pl.BlockSpec(memory_space=pl.ANY)
    vspec = pl.BlockSpec(memory_space=pltpu.VMEM)
    out = pl.pallas_call(
        functools.partial(kernel, ax_a, ax_b, na, nb, tok, width, heads, per),
        out_shape=jax.ShapeDtypeStruct((tok, width), BF16),
        in_specs=[anyspec, vspec, vspec, anyspec, anyspec, anyspec, anyspec, vspec],
        out_specs=vspec,
        scratch_shapes=[
            vm((tok, width), BF16),
            vm((width, wide), BF16),
            vm((width, wide), BF16),
            vm((width, wide), BF16),
            vm((wide, width), BF16),
            vm((8, 128), F32),
            vm((na * nb, 8, 128), F32),
            vm((na, gw, tok), BF16),
            vm((na - 1, gw, tok), BF16),
            vm((na, gw, tok), BF16),
            vm((na, vrows, 128), BF16),
            vm((na, nb, gw, tok), BF16),
            vm((na, nb, vrows, 128), BF16),
            vm((nb, tok, padw), BF16),
            vm((per, na, tok, HD), BF16),
            vm((per, na, tok, 128), F32),
            vm((per, na, tok, padw), F32),
            vm((na, gw, tok), BF16),
            vm((wide, tok), BF16),
            dma((5,)),
            dma((2,)),
            dma((na * nb,)),
            dma((na * nb,)),
            dma((na - 1,)),
            dma((na - 1,)),
            dma((na - 1, 2)),
            dma((na - 1, 2)),
            dma((na, nb, 2)),
            dma((na, nb, 2)),
            dma((na,)),
            dma((na,)),
        ],
        compiler_params=pltpu.CompilerParams(
            collective_id=0, has_side_effects=True, vmem_limit_bytes=56 * 1024 * 1024
        ),
    )(
        latent.reshape(tok, width), gain, shift, wq, wk, wv, wo, bias,
    )
    return out.reshape(rows, cols, width)


def solution(mesh):
    placed = (P(("img", "row"), "col", None), P(), P(), P(), P(), P(), P(), P())
    return jax.shard_map(
        functools.partial(local, dict(mesh.shape)),
        mesh=mesh, in_specs=placed, out_specs=P(("img", "row"), "col", None), check_vma=False,
    )
```

```python
import functools
import math

import jax
import jax.numpy as jnp
from jax import lax
from jax.experimental import pallas as pl
from jax.experimental.pallas import tpu as pltpu
from jax.sharding import PartitionSpec as P

GROUPS = 32
HD = 64
MESH = pl.DeviceIdType.MESH
F32 = jnp.float32
BF16 = jnp.bfloat16


def xor(a, s):
    out, bit = a, 1
    while bit <= s:
        if s & bit:
            out = out + bit * (1 - 2 * ((a // bit) % 2))
        bit *= 2
    return out


def xor_traced(a, s, n):
    out, bit = 0, 1
    while bit < n:
        out = out + bit * (((a // bit) + (s // bit)) % 2)
        bit *= 2
    return out


def kernel(
    ax_a, ax_b, na, nb, tok, width, wide_heads, per,
    x_hbm, gain_ref, shift_ref, wq_hbm, wk_hbm, wv_hbm, wo_hbm, bias_ref,
    out_ref,
    x_v, wq, wk, wv, wo, stat_own, stat_in, q_own, q_in, k_own, v_own, kbuf, vbuf, v_full, qh, m_s, acc, mix_out, mix_in,
    load_sem, own_sem, st_send, st_recv, q_send, q_recv, z_send, z_recv, f_send, f_recv, o_send, o_recv,
):
    me_a = lax.axis_index(ax_a)
    me_b = lax.axis_index(ax_b)
    gw = per * HD
    padw = v_full.shape[-1]
    whole, half_tok = gw // 128, tok // 2
    everyone = [(s, t) for s in range(na) for t in range(nb) if s or t]

    def dev(s, t):
        return {ax_a: xor(me_a, s), ax_b: xor(me_b, t)}

    def remote(src, dst, ssem, rsem, where):
        return pltpu.make_async_remote_copy(
            src_ref=src, dst_ref=dst, send_sem=ssem, recv_sem=rsem, device_id=where, device_id_type=MESH
        )

    loads = [
        pltpu.make_async_copy(a, b, load_sem.at[i])
        for i, (a, b) in enumerate(((x_hbm, x_v), (wq_hbm, wq), (wk_hbm, wk), (wv_hbm, wv), (wo_hbm, wo)))
    ]
    for copy in loads:
        copy.start()
    barrier = pltpu.get_barrier_semaphore()
    for s, t in everyone:
        pl.semaphore_signal(barrier, inc=1, device_id=dev(s, t), device_id_type=MESH)

    size = width // GROUPS
    chan = lax.broadcasted_iota(jnp.int32, (width, 128), 0)
    lane = lax.broadcasted_iota(jnp.int32, (width, 128), 1)
    gather = jnp.where((chan >= lane * size) & (chan < lane * size + size), 1.0, 0.0).astype(F32)
    chan_t = lax.broadcasted_iota(jnp.int32, (128, width), 1)
    lane_t = lax.broadcasted_iota(jnp.int32, (128, width), 0)
    spread = jnp.where((chan_t >= lane_t * size) & (chan_t < lane_t * size + size), 1.0, 0.0).astype(F32)

    def to_groups(row):
        return jnp.dot(
            jnp.broadcast_to(row, (8, width)), gather, preferred_element_type=F32, precision=lax.Precision.HIGHEST
        )[:1]

    def to_channels(row):
        return jnp.dot(
            jnp.broadcast_to(row, (8, 128)), spread, preferred_element_type=F32, precision=lax.Precision.HIGHEST
        )[:1]

    loads[0].wait()
    x = x_v[...].astype(F32)
    here = float(tok * size)
    mean_here = to_groups(jnp.sum(x, axis=0, keepdims=True)) / here
    off = x - to_channels(mean_here)
    dev_here = to_groups(jnp.sum(off * off, axis=0, keepdims=True))
    stat_own[...] = jnp.concatenate([mean_here, dev_here, jnp.zeros((6, 128), F32)], axis=0)
    pl.semaphore_wait(barrier, len(everyone))
    stats = []
    for s, t in everyone:
        i = s * nb + t
        copy = remote(stat_own, stat_in.at[i], st_send.at[i], st_recv.at[i], dev(s, t))
        copy.start()
        stats.append(copy)
    for copy in stats:
        copy.wait()
    means = [stat_own[0:1, :]] + [stat_in[s * nb + t, 0:1, :] for s, t in everyone]
    devs = [stat_own[1:2, :]] + [stat_in[s * nb + t, 1:2, :] for s, t in everyone]
    mean = sum(means) / float(na * nb)
    total_dev = sum(devs) + here * sum((m - mean) * (m - mean) for m in means)
    rstd = lax.rsqrt(total_dev / (here * na * nb) + 1e-05)
    both = jnp.dot(
        jnp.concatenate([mean, rstd, jnp.zeros((6, 128), F32)], axis=0), spread,
        preferred_element_type=F32, precision=lax.Precision.HIGHEST,
    )
    mean_c, rstd_c = both[0:1], both[1:2]
    normed = ((x_v[...].astype(F32) - mean_c) * rstd_c * gain_ref[...][None, :] + shift_ref[...][None, :]).astype(BF16)

    loads[1].wait()
    q = jnp.dot(normed, wq[...], preferred_element_type=F32) * (math.log2(math.e) / math.sqrt(HD))
    q = q.astype(BF16).astype(F32).T.astype(BF16)
    for g in range(na):
        q_own[g] = q[g * gw : (g + 1) * gw]
    q_copies = [
        remote(q_own.at[xor(me_a, s)], q_in.at[s - 1], q_send.at[s - 1], q_recv.at[s - 1], dev(s, 0))
        for s in range(1, na)
    ]
    for copy in reversed(q_copies):
        copy.start()
    loads[2].wait()
    k = jnp.dot(normed, wk[...], preferred_element_type=F32)
    k = k.astype(BF16).astype(F32).T.astype(BF16)
    for g in range(na):
        k_own[g] = k[g * gw : (g + 1) * gw]
    loads[3].wait()
    v = jnp.dot(normed, wv[...], preferred_element_type=F32)
    for g in range(na):
        part = v[:, g * gw : (g + 1) * gw].astype(BF16).astype(F32)
        for n in range(whole):
            v_own[g, n * tok : (n + 1) * tok, :] = part[:, n * 128 : (n + 1) * 128].astype(BF16)
        rest = part[:, whole * 128 :]
        folded = jnp.concatenate([rest[:half_tok], rest[half_tok:]], axis=1)
        v_own[g, whole * tok :, :] = folded.astype(BF16)
    owned, landed = (k_own, v_own), (kbuf, vbuf)

    def exchange(s, p):
        return remote(
            owned[p].at[xor(me_a, s)], landed[p].at[s, 0], z_send.at[s - 1, p], z_recv.at[s - 1, p], dev(s, 0)
        )

    for p in range(2):
        for s in (3, 1):
            exchange(s, p).start()
    own = [pltpu.make_async_copy(owned[p].at[me_a], landed[p].at[0, 0], own_sem.at[p]) for p in range(2)]
    for copy in own:
        copy.start()

    def forward(s, t, p):
        buf = landed[p]
        src = buf.at[s, t - 1] if t % 2 and t > 1 else buf.at[s, 0]
        hop = 1 if t % 2 else t
        return remote(src, buf.at[s, t], f_send.at[s, t, p], f_recv.at[s, t, p], dev(0, hop))

    direct = [t for t in range(1, nb) if t == 1 or t % 2 == 0]
    relayed = [t for t in range(3, nb, 2)]

    def first(s):
        for p in range(2):
            if s == 0:
                own[p].wait()
            else:
                exchange(s, p).wait_recv()
            for t in reversed(direct):
                forward(s, t, p).start()

    def second(s):
        for p in range(2):
            for t in relayed:
                forward(s, t - 1, p).wait_recv()
                forward(s, t, p).start()

    def third(s):
        for t in range(nb):
            for p in range(2):
                if t and t + 1 not in relayed:
                    forward(s, t, p).wait_recv()
            for n in range(whole):
                v_full[t, :, n * 128 : (n + 1) * 128] = vbuf[s, t, n * tok : (n + 1) * tok, :]
            folded = vbuf[s, t, whole * tok :, :].astype(F32)
            lower = jnp.concatenate([folded[:, :HD], jnp.ones((half_tok, 128 - HD), F32)], axis=1)
            upper = jnp.concatenate([folded[:, HD:], jnp.ones((half_tok, 128 - HD), F32)], axis=1)
            v_full[t, :half_tok, whole * 128 :] = lower.astype(BF16)
            v_full[t, half_tok:, whole * 128 :] = upper.astype(BF16)

    def unpack(i, block):
        for h in range(per):
            qh[h, i] = block[h * HD : (h + 1) * HD].astype(F32).T.astype(BF16)

    def score(s, i, h):
        query = qh[h, i]
        return [
            jnp.dot(query, kbuf[s, t, h * HD : (h + 1) * HD, :], preferred_element_type=F32) for t in range(nb)
        ]

    def absorb(s, i, h, scores):
        peak = functools.reduce(jnp.maximum, scores)
        peak = jnp.max(peak, axis=1, keepdims=True)
        if s:
            old = m_s[h, i][:, :1]
            peak = jnp.maximum(peak, old)
        mixed = None
        for t in range(nb):
            rounded = jnp.exp2(scores[t] - peak).astype(BF16)
            piece = jnp.dot(rounded, v_full[t], preferred_element_type=F32)
            mixed = piece if mixed is None else mixed + piece
        if s:
            mixed = acc[h, i] * jnp.exp2(old - peak) + mixed
        acc[h, i] = mixed
        if s != last:
            m_s[h, i] = jnp.broadcast_to(peak, (tok, 128))

    def compute(s, i):
        scores = score(s, i, 0)
        for h in range(per):
            later = score(s, i, h + 1) if h + 1 < per else None
            absorb(s, i, h, scores)
            scores = later

    def run(s, low, high):
        lax.fori_loop(low, high, lambda i, c: (compute(s, i), c)[1], 0)

    def finish(i):
        parts = []
        for h in range(per):
            a = acc[h, i]
            parts.append(a[:, h * HD : (h + 1) * HD] / a[:, gw : gw + 1])
        return jnp.concatenate(parts, axis=1).astype(BF16).astype(F32).T.astype(BF16)

    last = 2
    first(0)
    unpack(0, q_own[me_a])
    second(0)
    third(0)
    run(0, 0, 1)
    for i in range(1, na):
        q_copies[i - 1].wait()
        unpack(i, q_in[i - 1])
    run(0, 1, 2)
    first(1)
    run(0, 2, 3)
    first(3)
    for p in range(2):
        exchange(2, p).start()
    second(1)
    run(0, 3, 4)
    second(3)
    third(1)
    run(1, 0, 4)
    first(2)
    third(3)
    run(3, 0, 2)
    second(2)
    run(3, 2, 4)
    third(2)

    def back(j, c):
        i = na - 1 - j
        compute(last, i)
        mix_out[i] = finish(i)
        remote(
            mix_out.at[i],
            mix_in.at[pl.ds(pl.multiple_of(me_a * gw, gw), gw)],
            o_send.at[i],
            o_recv.at[i],
            {ax_a: xor_traced(me_a, i, na), ax_b: me_b},
        ).start()
        return c

    lax.fori_loop(0, na - 1, back, 0)
    compute(last, 0)
    mix_in[pl.ds(pl.multiple_of(me_a * gw, gw), gw), :] = finish(0)
    loads[4].wait()
    for p in range(2):
        for s in range(na):
            if s:
                exchange(s, p).wait_send()
            for t in range(1, nb):
                forward(s, t, p).wait_send()
    for i in range(1, na):
        copy = remote(
            mix_out.at[i],
            mix_in.at[pl.ds(pl.multiple_of(xor(me_a, i) * gw, gw), gw)],
            o_send.at[i],
            o_recv.at[i],
            dev(i, 0),
        )
        copy.wait()
    mixed = mix_in[...].astype(F32).T.astype(BF16)
    result = jnp.dot(mixed, wo[...], preferred_element_type=F32) + bias_ref[...][None, :]
    out_ref[...] = result.astype(BF16)


def local(sizes, latent, gain, shift, wq, wk, wv, wo, bias):
    rows, cols, width = latent.shape
    tok = rows * cols
    wide = wq.shape[1]
    heads = wide // HD
    ax_a, ax_b = ("row", "col") if heads % sizes["row"] == 0 else ("col", "row")
    na, nb = sizes[ax_a], sizes[ax_b]
    per = heads // na
    gw = per * HD
    padw = (gw // 128 + 1) * 128
    assert na == 4 and gw % 128 == HD
    vrows = tok * (gw // 128) + tok // 2
    vm = pltpu.VMEM
    dma = pltpu.SemaphoreType.DMA
    anyspec = pl.BlockSpec(memory_space=pl.ANY)
    vspec = pl.BlockSpec(memory_space=pltpu.VMEM)
    out = pl.pallas_call(
        functools.partial(kernel, ax_a, ax_b, na, nb, tok, width, heads, per),
        out_shape=jax.ShapeDtypeStruct((tok, width), BF16),
        in_specs=[anyspec, vspec, vspec, anyspec, anyspec, anyspec, anyspec, vspec],
        out_specs=vspec,
        scratch_shapes=[
            vm((tok, width), BF16),
            vm((width, wide), BF16),
            vm((width, wide), BF16),
            vm((width, wide), BF16),
            vm((wide, width), BF16),
            vm((8, 128), F32),
            vm((na * nb, 8, 128), F32),
            vm((na, gw, tok), BF16),
            vm((na - 1, gw, tok), BF16),
            vm((na, gw, tok), BF16),
            vm((na, vrows, 128), BF16),
            vm((na, nb, gw, tok), BF16),
            vm((na, nb, vrows, 128), BF16),
            vm((nb, tok, padw), BF16),
            vm((per, na, tok, HD), BF16),
            vm((per, na, tok, 128), F32),
            vm((per, na, tok, padw), F32),
            vm((na, gw, tok), BF16),
            vm((wide, tok), BF16),
            dma((5,)),
            dma((2,)),
            dma((na * nb,)),
            dma((na * nb,)),
            dma((na - 1,)),
            dma((na - 1,)),
            dma((na - 1, 2)),
            dma((na - 1, 2)),
            dma((na, nb, 2)),
            dma((na, nb, 2)),
            dma((na,)),
            dma((na,)),
        ],
        compiler_params=pltpu.CompilerParams(
            collective_id=0, has_side_effects=True, vmem_limit_bytes=56 * 1024 * 1024
        ),
    )(
        latent.reshape(tok, width), gain, shift, wq, wk, wv, wo, bias,
    )
    return out.reshape(rows, cols, width)


def solution(mesh):
    placed = (P(("img", "row"), "col", None), P(), P(), P(), P(), P(), P(), P())
    return jax.shard_map(
        functools.partial(local, dict(mesh.shape)),
        mesh=mesh, in_specs=placed, out_specs=P(("img", "row"), "col", None), check_vma=False,
    )
```
